128 devices in a mesh: span: 32 (over z, x, core), chord: 4 (over y).
Axes of the slice: x: 4, y: 4, z: 4, core: 2. Of those that a mesh axis runs over, the one named last changes fastest.
Arguments:
- surface_adjoint: bfloat16 [128, 2048, 2, 384], P('chord', 'span'), may hold values from -6 to 6
- velocity_adjoint: bfloat16 [2, 128, 2048, 2, 384], P(None, 'chord', 'span'), may hold values from -6 to 6
- metric: float32 [2, 128, 2048], P(None, 'chord', 'span'), may hold values from 0.5 to 2
- aic_blocks: bfloat16 [16, 128, 8, 2, 128, 128], P('chord', 'span'), may hold values from -0.125 to 0.125
- block_codes: int32 [16, 128, 8], P('chord', 'span'), may hold values from 0 to 8, all different within a row
- wake_adjoint: bfloat16 [65536, 2, 384], P(('span', 'chord')), may hold values from -3 to 3
- wake_owner: int32 [65536, 1], P(('span', 'chord')), may hold values from 0 to 31; in each aligned block of 512 rows (0 to 511, 512 to 1023, ...) at most 32 rows name the same one
- shed_station: int32 [65536], P(('span', 'chord')), may hold values from 0 to 63
Outputs:
- surface_out: bfloat16 [128, 2048, 2, 384], P('chord', 'span')
The draws below stay inside these ranges and needn't reach their ends.
Inputs may be any that keep to these rules, and one draw needn't show every extreme that they name: `block_codes`: the 8 codes of one block are distinct. `wake_owner`: among the wake panels of one device no span index is named more than 32 times, and in some device one span index is named exactly 32 times.
All inputs are finite; a program needn't handle non-finite values.
Results may differ from the reference program's by a relative error of at most 0.0041.
Values may be sent and summed in bfloat16 or wider, within the bound.
No kernel may reach another device: no remote copies, remote signals or barrier semaphores. Data moves between devices by JAX's collectives and lax.ppermute only.
A program may use at most 256 MiB of HBM per device.

```python
import math
import jax
import jax.numpy as jnp
import numpy as np
from jax import lax

BC = 8
BS = 16
BLK = 128
R = 384
K = 8
SBK = 4
W_DEV = 512
NCB = 16
NSB = 128
NC = 128
NS = 2048
PS = 64
W_TOT = 65536
CAP = 32
N_SPAN = 32


def touch_ends(array, key, least, high):
    longest = array.shape.index(max(array.shape))
    spots = []
    for shift in (0, 1):
        where = [jax.random.randint(jax.random.fold_in(key, axis), (), 0, length) for axis, length in enumerate(array.shape)]
        where[longest] = (where[longest] + shift) % array.shape[longest]
        spots.append(tuple(where))
    return array.at[spots[0]].set(least).at[spots[1]].set(high)


def block_scale(own_key, extent, split, least, top_value):
    def one(dim, blocks):
        steps = jax.random.uniform(jax.random.fold_in(jax.random.fold_in(own_key, 6), dim), (blocks,), jnp.float32, least / len(split), top_value / len(split))
        return jnp.repeat(jnp.exp(steps), extent[dim] // blocks).reshape((-1,) + (1,) * (len(extent) - dim - 1))

    factor_of = one(*split[0])
    for cut in split[1:]:
        factor_of = factor_of * one(*cut)
    return factor_of


def distinct(rng, rows, amount, top, lift):
    order = jax.random.permutation(jax.random.fold_in(rng, 1), amount)
    pull = order
    for power in range(3):
        pull = pull * pull // amount
    pull = pull * lift // amount
    chance = jax.random.randint(jax.random.fold_in(rng, 2), (rows, amount), 0, 4096) + pull
    holders = jax.random.permutation(jax.random.fold_in(rng, 3), rows)[jnp.arange(amount) % rows]
    chance = jnp.where(jnp.arange(rows)[:, None] == holders[None, :], 1 << 14, chance)
    score = chance * amount + jnp.arange(amount)
    return lax.top_k(score.astype(jnp.int32), top)[1].astype(jnp.int32)


def shared_out(own_key, own, number, rows, amount, top, limit, slope):
    order = jax.random.permutation(own_key, amount)
    crowded, ordinary = shares(amount, rows * top, limit, slope, True), shares(amount, rows * top, limit, slope, False)
    places = jnp.arange(amount)

    def named(lengths, rotation):
        used = int((lengths > 0).sum())
        fixed = max(1, used // 4)
        moved = fixed + (places - fixed + rotation * (used - fixed)) % max(1, amount - fixed)
        return jnp.zeros((amount,), jnp.int32).at[order[jnp.where(places < fixed, places, moved)]].set(jnp.asarray(lengths, jnp.int32))

    lengths = jnp.where(number % 4 == 0, named(crowded, number // 4), named(ordinary, number - number // 4 - 1))
    mixed = jax.random.permutation(jax.random.fold_in(own, 3), amount)
    source_of, taker = mixed[0:amount // 2 * 2:2], mixed[1:amount // 2 * 2:2]
    margin = jnp.minimum(lengths[source_of] - 1, limit - lengths[taker]) // 2
    margin = jnp.where((source_of == order[0]) | (taker == order[0]) | (lengths[taker] == 0), 0, jnp.maximum(margin, 0))
    moved = jax.random.randint(jax.random.fold_in(own, 4), (amount // 2,), 0, 1 << 20) % (margin + 1)
    lengths = lengths.at[source_of].add(-moved).at[taker].add(moved)
    labels = jnp.searchsorted(jnp.cumsum(lengths), jnp.arange(rows * top), side="right").astype(jnp.int32)
    grid = labels.reshape(top, rows).T
    grid = grid[jax.random.permutation(jax.random.fold_in(own, 1), rows)]
    rotation = jax.random.randint(jax.random.fold_in(own, 2), (rows, 1), 0, top)
    return jnp.take_along_axis(grid, (jnp.arange(top)[None, :] + rotation) % top, axis=1)


def shares(amount, total, bound, skew, full):
    weights = [(1 << 20) // math.isqrt(rank ** skew) + 1 for rank in range(1, amount + 1)]
    largest = bound if full else min(bound, max(-(-total // amount), total * weights[0] // sum(weights)))
    least = 1 if total - largest >= amount - 1 else 0
    given, rest = [largest] + [least] * (amount - 1), total - largest - least * (amount - 1)
    while rest > 0:
        free = [i for i in range(1, amount) if given[i] < largest] or [i for i in range(1, amount) if given[i] < bound]
        mass, budget = sum([weights[i] for i in free]), rest
        for i in free:
            extra = min(bound - given[i], max(1, budget * weights[i] // mass), rest)
            given[i] = given[i] + extra
            rest = rest - extra
    return np.array(given)


def normal_values(own_key, extent, width, most, shards=(), held_as=jnp.bfloat16):
    array = width * jax.random.normal(own_key, extent, jnp.float32)
    if shards:
        array = array * block_scale(own_key, extent, shards, -0.22, 0.18)
    return jnp.clip(array, -most, most).astype(held_as)


def setup_inputs(seed: int = 0) -> dict:
    splits = jax.random.split(jax.random.key(seed), 9)
    surface_adjoint = normal_values(splits[0], (NC, NS, 2, R), 1.0, 6.0, ((0, 4), (1, 32)))
    velocity_adjoint = normal_values(splits[1], (2, NC, NS, 2, R), 1.0, 6.0, ((1, 4), (2, 32)))
    metric = jnp.clip(jnp.exp(math.log(2.0) - 1.3862944 * jax.random.uniform(splits[2], (2, NC, NS), jnp.float32) ** block_scale(splits[2], (2, NC, NS), ((1, 4), (2, 32)), -0.2, 0.2)), 0.5, 2.0)
    aic_blocks = normal_values(splits[3], (NCB, NSB, K, 2, BLK, BLK), (2 * K * BLK) ** -0.5, 0.125, ((0, 4), (1, 32)))
    block_codes = distinct(splits[4], NCB * NSB, 9, K, 0).reshape((NCB, NSB, K))
    wake_adjoint = normal_values(splits[5], (W_TOT, 2, R), 0.2, 3.0, ((0, 128),))
    wake_owner_keys = jax.random.split(jax.random.fold_in(splits[6], 1), W_TOT // W_DEV)
    wake_owner_turns = jax.random.permutation(jax.random.fold_in(splits[6], 3), W_TOT // W_DEV)
    wake_owner = jax.vmap(lambda own, number: shared_out(jax.random.fold_in(splits[6], 2), own, number, W_DEV, N_SPAN, 1, CAP, 2))(wake_owner_keys, wake_owner_turns).reshape((W_TOT, 1))
    shed_station = touch_ends(jax.random.randint(splits[7], (W_TOT,), 0, PS), jax.random.fold_in(splits[7], 1), 0, PS - 1).astype(jnp.int32)
    return {"surface_adjoint": surface_adjoint, "velocity_adjoint": velocity_adjoint, "metric": metric, "aic_blocks": aic_blocks, "block_codes": block_codes, "wake_adjoint": wake_adjoint, "wake_owner": wake_owner, "shed_station": shed_station}


def to_blocks(surface, block_rows, block_cols):
    shaped = surface.reshape(block_rows, BC, block_cols, BS, 2, R)
    shaped = jnp.transpose(shaped, (0, 2, 1, 3, 4, 5))
    return shaped.reshape(block_rows, block_cols, BC * BS, 2, R)


def from_blocks(blocks, block_rows, block_cols):
    shaped = blocks.reshape(block_rows, block_cols, BC, BS, 2, R)
    shaped = jnp.transpose(shaped, (0, 2, 1, 3, 4, 5))
    return shaped.reshape(block_rows * BC, block_cols * BS, 2, R)


def near_sum(flat_blocks, gather_index, matrices):
    block_count = gather_index.shape[0]
    real_sum = jnp.zeros((block_count, BC * BS, R), jnp.float32)
    imag_sum = jnp.zeros((block_count, BC * BS, R), jnp.float32)
    for slot_index in range(K):
        sources = flat_blocks[gather_index[:, slot_index]].astype(jnp.float32)
        matrix = matrices[:, slot_index].astype(jnp.float32)
        real_sum = real_sum + jnp.einsum("bpq,bqr->bpr", matrix[:, 0], sources[:, :, 0]) - jnp.einsum("bpq,bqr->bpr", matrix[:, 1], sources[:, :, 1])
        imag_sum = imag_sum + jnp.einsum("bpq,bqr->bpr", matrix[:, 0], sources[:, :, 1]) + jnp.einsum("bpq,bqr->bpr", matrix[:, 1], sources[:, :, 0])
    return jnp.stack([real_sum, imag_sum], axis=2)


def reference(surface_adjoint, velocity_adjoint, metric, aic_blocks, block_codes, wake_adjoint, wake_owner, shed_station):
    blocks = to_blocks(surface_adjoint, NCB, NSB)
    padded = jnp.pad(blocks, ((1, 1), (1, 1), (0, 0), (0, 0), (0, 0)))
    columns = jnp.arange(NSB, dtype=jnp.int32)[:, None]

    def one_row(row_number):
        strip_blocks = lax.dynamic_slice_in_dim(padded, row_number, 3, 0).reshape(3 * (NSB + 2), BC * BS, 2, R)
        row_codes = lax.dynamic_index_in_dim(block_codes, row_number, 0, keepdims=False)
        row_matrices = lax.dynamic_index_in_dim(aic_blocks, row_number, 0, keepdims=False)
        gather_index = ((row_codes // 3) * (NSB + 2) + columns + row_codes % 3).astype(jnp.int32)
        return near_sum(strip_blocks, gather_index, row_matrices)

    near_field = lax.map(one_row, jnp.arange(NCB, dtype=jnp.int32))
    near_field = from_blocks(near_field, NCB, NSB)

    weighted = (metric[:, :, :, None, None] * velocity_adjoint.astype(jnp.float32)).astype(jnp.bfloat16)
    padded_weights = jnp.pad(weighted, ((0, 0), (1, 1), (1, 1), (0, 0), (0, 0))).astype(jnp.float32)
    gradient = 0.5 * (padded_weights[0, :-2, 1:-1] - padded_weights[0, 2:, 1:-1]) + 0.5 * (padded_weights[1, 1:-1, :-2] - padded_weights[1, 1:-1, 2:])

    station = (wake_owner[:, 0] * (SBK * BS) + shed_station).astype(jnp.int32)
    shed_sum = jax.ops.segment_sum(wake_adjoint.astype(jnp.float32), station, num_segments=NS)

    summed = near_field + gradient
    summed = summed.at[0].add(-shed_sum).at[NC - 1].add(shed_sum)
    return summed.astype(jnp.bfloat16)
```

```python
import jax
import jax.numpy as jnp
from jax import lax
from jax.experimental import pallas as pl
from jax.experimental.pallas import tpu as pltpu
from jax.sharding import PartitionSpec as P

BC = 8
BS = 16
R = 384
CAP = 32
LANES = 128
META = 192
ROWS = 208
F32 = jnp.float32
BF16 = jnp.bfloat16


def split_parts(array):
    return jnp.swapaxes(array, -3, -2)


def shift(array, axis, step):
    count = lax.axis_size(axis)
    pairs = [(i, i + step) for i in range(count) if 0 <= i + step < count]
    return lax.ppermute(array, axis, pairs)


def pack_kernel(owner_ref, station_ref, wake_ref, out_ref):
    rows = owner_ref.shape[1]
    owners = out_ref.shape[0]
    owner = owner_ref[...]
    station = station_ref[...]
    named = lax.broadcasted_iota(jnp.int32, (owners, rows), 0) == owner
    hot = jnp.where(named, 1.0, 0.0).astype(F32)
    before = jnp.where(
        lax.broadcasted_iota(jnp.int32, (rows, rows), 0)
        < lax.broadcasted_iota(jnp.int32, (rows, rows), 1),
        1.0,
        0.0,
    ).astype(BF16)
    counts = jnp.dot(hot.astype(BF16), before, preferred_element_type=F32)
    rank = jnp.sum(hot * counts, axis=0, keepdims=True).astype(jnp.int32)
    slot = owner * CAP + rank
    stations = jnp.where(named, (station + 1).astype(F32), 0.0).astype(BF16)
    ranks = jnp.where(
        lax.broadcasted_iota(jnp.int32, (LANES, rows), 0) == rank, 1.0, 0.0
    ).astype(BF16)
    meta = lax.dot_general(
        stations, ranks, (((1,), (1,)), ((), ())), preferred_element_type=F32
    ).astype(BF16)
    for d in range(owners):
        out_ref[d, META:ROWS, :] = jnp.broadcast_to(meta[d : d + 1], (ROWS - META, LANES))
    values = jnp.concatenate([wake_ref[0], wake_ref[1]], axis=1)
    chunk = 256
    for first in range(0, owners * CAP, chunk):
        place = jnp.where(
            lax.broadcasted_iota(jnp.int32, (chunk, rows), 0) + first == slot, 1.0, 0.0
        ).astype(BF16)
        packed = jnp.dot(place, values, preferred_element_type=F32).astype(BF16)
        for d in range(chunk // CAP):
            for part in range(6):
                out_ref[first // CAP + d, part * CAP : (part + 1) * CAP, :] = packed[
                    d * CAP : (d + 1) * CAP, part * LANES : (part + 1) * LANES
                ]


def pack(owner, station, wake, owners):
    return pl.pallas_call(
        pack_kernel,
        out_shape=jax.ShapeDtypeStruct((owners, ROWS, LANES), BF16),
        compiler_params=pltpu.CompilerParams(vmem_limit_bytes=32 * 1024 * 1024),
        name="wake_pack",
    )(owner, station, wake)


def sum_kernel(got_ref, out_ref):
    sources = got_ref.shape[0]
    width = out_ref.shape[1]
    group = LANES // CAP
    total = jnp.zeros((width, 6 * LANES), F32)
    for first in range(0, sources, 2 * group):
        hots, values = [], []
        for half in range(2):
            base = first + half * group
            codes = jnp.zeros((ROWS - META, LANES), F32)
            for q in range(group):
                row = got_ref[base + q, META:ROWS, :].astype(F32)
                codes = codes + (pltpu.roll(row, q * CAP, axis=1) if q else row)
            wanted = lax.broadcasted_iota(jnp.int32, (width, LANES), 0).astype(F32) + 1.0
            hots.append(jnp.where(codes[0:1] == wanted, 1.0, 0.0).astype(BF16))
            values.append(
                jnp.concatenate(
                    [
                        got_ref[base : base + group, part * CAP : (part + 1) * CAP, :].reshape(
                            LANES, LANES
                        )
                        for part in range(6)
                    ],
                    axis=1,
                )
            )
        total = total + jnp.dot(
            jnp.concatenate(hots, axis=1),
            jnp.concatenate(values, axis=0),
            preferred_element_type=F32,
        )
    out_ref[0] = total[:, :R]
    out_ref[1] = total[:, R:]


def sum_stations(got, width):
    return pl.pallas_call(
        sum_kernel,
        out_shape=jax.ShapeDtypeStruct((2, width, R), F32),
        compiler_params=pltpu.CompilerParams(vmem_limit_bytes=32 * 1024 * 1024),
        name="wake_sum",
    )(got)


def surface_kernel(
    first_row,
    codes_ref,
    place_ref,
    own0_ref,
    own1_ref,
    own2_ref,
    chord_ref,
    inner_ref,
    outer_ref,
    inner_corner_ref,
    outer_corner_ref,
    aic_ref,
    down_ref,
    before_ref,
    after_ref,
    along_ref,
    metric_ref,
    *rest,
):
    out_ref, blocks, weights, spread, gradient, rim = rest[-6:]
    step = pl.program_id(0)
    steps = pl.num_programs(0)
    t = first_row + step
    cols = own0_ref.shape[2]
    bcols = cols // BS
    last = metric_ref.shape[1] - 1
    even = place_ref[0] == 0
    upper = first_row == 0

    @pl.when(step == 0)
    def _():
        def put(r, q, source, row, col):
            for part in range(2):
                for a in range(BC):
                    blocks[r, q, part, a * BS : (a + 1) * BS, :] = source[
                        row + a, part, col : col + BS, :
                    ]

        shift_row = 1 if upper else 0
        edge = 0 if upper else 3
        for q in range(bcols):
            put(edge, q + 1, chord_ref, 0, q * BS)
            for r, source in enumerate((own0_ref, own1_ref, own2_ref)):
                put(r + shift_row, q + 1, source, 0, q * BS)

        def sides(left, right, left_corner, right_corner):
            base = 0 if upper else BC
            put(edge, 0, left_corner, base, 0)
            put(edge, bcols + 1, right_corner, base, 0)
            for r in range(3):
                put(r + shift_row, 0, left, base + r * BC, 0)
                put(r + shift_row, bcols + 1, right, base + r * BC, 0)
            line = left.shape[0] - 2 + (0 if upper else 1)
            rim[0] = left[line].astype(F32)
            rim[1] = right[line].astype(F32)

        @pl.when(even)
        def _():
            sides(outer_ref, inner_ref, outer_corner_ref, inner_corner_ref)

        @pl.when(jnp.logical_not(even))
        def _():
            sides(inner_ref, outer_ref, inner_corner_ref, outer_corner_ref)

    diagonal = lax.broadcasted_iota(jnp.int32, (cols, cols), 0) == lax.broadcasted_iota(
        jnp.int32, (cols, cols), 1
    )

    def factor(component, i):
        line = metric_ref[component, pl.ds(i, 1), :]
        return jnp.sum(jnp.where(diagonal, line, 0.0), axis=1, keepdims=True)

    def weigh(value, column):
        return (value.astype(F32) * column).astype(BF16)

    def weigh_row(a, carry):
        column = factor(0, t * BC + a)
        for part in range(2):
            weights[a + 1, part] = weigh(down_ref[0, a, part], column)
        return carry

    lax.fori_loop(0, BC, weigh_row, 0, unroll=2)
    if upper:

        @pl.when(step == 0)
        def _():
            weights[0] = chord_ref[BC]

        @pl.when(step > 0)
        def _():
            column = factor(0, t * BC - 1)
            for part in range(2):
                weights[0, part] = weigh(before_ref[0, 0, part], column)

        column = factor(0, t * BC + BC)
        for part in range(2):
            weights[BC + 1, part] = weigh(after_ref[0, 0, part], column)
    else:

        @pl.when(step == steps - 1)
        def _():
            weights[BC + 1] = chord_ref[BC]

        @pl.when(step < steps - 1)
        def _():
            column = factor(0, t * BC + BC)
            for part in range(2):
                weights[BC + 1, part] = weigh(after_ref[0, 0, part], column)

        column = factor(0, t * BC - 1)
        for part in range(2):
            weights[0, part] = weigh(before_ref[0, 0, part], column)

    def slope_row(a, carry):
        column = factor(1, t * BC + a)
        for part in range(2):
            spread[part, 8 : 8 + cols, :] = weigh(along_ref[0, a, part], column).astype(F32)
            spread[part, 7:8, :] = rim[0, part, pl.ds(step * BC + a, 1), :]
            spread[part, 8 + cols : 9 + cols, :] = rim[1, part, pl.ds(step * BC + a, 1), :]
        for part in range(2):
            along = spread[part, 7 : 7 + cols, :] - spread[part, 9 : 9 + cols, :]
            down = weights[a, part].astype(F32) - weights[a + 2, part].astype(F32)
            gradient[a, part] = 0.5 * (down + along)
        return carry

    lax.fori_loop(0, BC, slope_row, 0, unroll=2)

    def target(u, carry):
        col = pl.multiple_of(u * BS, BS)
        for c in range(R // LANES):
            lanes = slice(c * LANES, (c + 1) * LANES)
            total = jnp.zeros((BC * BS, 2 * LANES), F32)
            for k in range(aic_ref.shape[2]):
                code = codes_ref[t, u, k]
                r = step + code // 3
                q = u + code % 3
                real = blocks[r, q, 0, :, lanes]
                imag = blocks[r, q, 1, :, lanes]
                source = jnp.concatenate(
                    [
                        jnp.concatenate([real, imag], axis=1),
                        jnp.concatenate([-imag, real], axis=1),
                    ],
                    axis=0,
                )
                matrix = jnp.concatenate([aic_ref[0, u, k, 0], aic_ref[0, u, k, 1]], axis=1)
                total = total + jnp.dot(matrix, source, preferred_element_type=F32)
            for a in range(BC):
                for part in range(2):
                    near = total[a * BS : (a + 1) * BS, part * LANES : (part + 1) * LANES]
                    slope = gradient[a, part, pl.ds(col, BS), lanes]
                    out_ref[a, part, pl.ds(col, BS), lanes] = (near + slope).astype(BF16)
        return carry

    lax.fori_loop(0, bcols, target, 0)


def surface(
    half, codes, place, own, chord, inner, outer, inner_corner, outer_corner, aic, velocity,
    metric, done=None,
):
    rows, _, cols, _ = own.shape
    brows, bcols = rows // BC, cols // BS
    steps = brows // 2
    first = half * steps
    whole = pl.BlockSpec(memory_space=pltpu.VMEM)
    scalars = pl.BlockSpec(memory_space=pltpu.SMEM)
    line = (1, 1, 2, cols, R)

    def strip(j):
        return pl.BlockSpec((BC, 2, cols, R), lambda s: (half + j, 0, 0, 0))

    arguments = [
        codes, place, own, own, own, chord, inner, outer, inner_corner, outer_corner, aic,
        velocity, velocity, velocity, velocity, metric,
    ]
    specs = (
        [scalars] * 2
        + [strip(j) for j in range(3)]
        + [whole] * 5
        + [
            pl.BlockSpec((1,) + aic.shape[1:], lambda s: (first + s, 0, 0, 0, 0, 0)),
            pl.BlockSpec((1, BC, 2, cols, R), lambda s: (0, first + s, 0, 0, 0)),
            pl.BlockSpec(line, lambda s: (0, jnp.maximum((first + s) * BC - 1, 0), 0, 0, 0)),
            pl.BlockSpec(
                line, lambda s: (0, jnp.minimum((first + s) * BC + BC, rows - 1), 0, 0, 0)
            ),
            pl.BlockSpec((1, BC, 2, cols, R), lambda s: (1, first + s, 0, 0, 0)),
            whole,
        ]
    )
    aliases = {}
    if done is not None:
        aliases = {len(arguments): 0}
        arguments.append(done)
        specs.append(pl.BlockSpec(memory_space=pl.ANY))

    def kernel(*refs):
        surface_kernel(first, *refs)

    return pl.pallas_call(
        kernel,
        grid=(steps,),
        in_specs=specs,
        out_specs=pl.BlockSpec((BC, 2, cols, R), lambda s: (first + s, 0, 0, 0)),
        out_shape=jax.ShapeDtypeStruct(own.shape, BF16),
        scratch_shapes=[
            pltpu.VMEM((4, bcols + 2, 2, BC * BS, R), BF16),
            pltpu.VMEM((BC + 2, 2, cols, R), BF16),
            pltpu.VMEM((2, cols + 16, R), F32),
            pltpu.VMEM((BC, 2, cols, R), F32),
            pltpu.VMEM((2, 2, 2 * BC, R), F32),
        ],
        input_output_aliases=aliases,
        compiler_params=pltpu.CompilerParams(vmem_limit_bytes=40 * 1024 * 1024),
        cost_estimate=pl.CostEstimate(
            flops=3_250_000_000, bytes_accessed=14_000_000, transcendentals=0
        ),
        name="surface_upper" if half == 0 else "surface_lower",
    )(*arguments)


def per_device(
    surface_adjoint,
    velocity_adjoint,
    metric,
    aic_blocks,
    block_codes,
    wake_adjoint,
    wake_owner,
    shed_station,
):
    rows, cols = surface_adjoint.shape[:2]
    owners = lax.axis_size("span")
    core = lax.axis_index("span") % 2
    own = split_parts(surface_adjoint)

    def weigh(factor, value):
        return (factor[..., None, None] * value.astype(F32)).astype(BF16)

    up_row = split_parts(weigh(metric[0, rows - 1], velocity_adjoint[0, rows - 1]))
    down_row = split_parts(weigh(metric[0, 0], velocity_adjoint[0, 0]))
    up_send = jnp.concatenate([own[rows - BC :], up_row[None]], axis=0)
    down_send = jnp.concatenate([own[:BC], down_row[None]], axis=0)
    up_send, down_send, wake, velocity_adjoint = lax.optimization_barrier(
        (up_send, down_send, wake_adjoint, velocity_adjoint)
    )
    low = shift(up_send, "chord", 1)
    high = shift(down_send, "chord", -1)

    packed = pack(
        wake_owner.reshape(1, -1), shed_station.reshape(1, -1), jnp.swapaxes(wake, 0, 1), owners
    )
    got = lax.all_to_all(packed, "span", 0, 0, tiled=True)

    inner_pairs = [(i, i ^ 1) for i in range(owners)]
    outer_pairs = [(i, i + 1) for i in range(1, owners - 1, 2)]
    outer_pairs = outer_pairs + [(j, i) for i, j in outer_pairs]
    inner_col = (1 - core) * (cols - BS)
    outer_col = core * (cols - BS)

    def side(first_col, lone_col):
        strip = lax.dynamic_slice_in_dim(own, first_col, BS, axis=2)
        lone = lax.dynamic_index_in_dim(velocity_adjoint[1], lone_col, axis=1, keepdims=False)
        scale = lax.dynamic_index_in_dim(metric[1], lone_col, axis=1, keepdims=False)
        lone = split_parts(weigh(scale, lone).reshape(rows // BS, BS, 2, R))
        return jnp.concatenate([strip, lone], axis=0)

    inner = lax.ppermute(side(inner_col, (1 - core) * (cols - 1)), "span", inner_pairs)
    outer = lax.ppermute(side(outer_col, core * (cols - 1)), "span", outer_pairs)

    def corner(first_col):
        return jnp.concatenate(
            [lax.dynamic_slice_in_dim(ref[:BC], first_col, BS, axis=2) for ref in (low, high)],
            axis=0,
        )

    inner_corner = lax.ppermute(corner(inner_col), "span", inner_pairs)
    outer_corner = lax.ppermute(corner(outer_col), "span", outer_pairs)
    velocity = split_parts(velocity_adjoint)
    place = jnp.full((1,), core, jnp.int32)
    halos = (inner, outer, inner_corner, outer_corner, aic_blocks, velocity, metric)
    summed = surface(0, block_codes, place, own, low, *halos)
    summed = surface(1, block_codes, place, own, high, *halos, done=summed)
    out = lax.optimization_barrier(split_parts(summed))

    partial = sum_stations(got, cols)
    count = lax.axis_size("chord")
    place = lax.axis_index("chord")
    half = count // 2
    pairs = [(i, 0 if i < half else count - 1) for i in (1, count - 2)]
    partial = partial + lax.ppermute(partial.astype(BF16), "chord", pairs).astype(F32)
    swap = [(0, count - 1), (count - 1, 0)]
    shed = partial + lax.ppermute(partial.astype(BF16), "chord", swap).astype(F32)
    shed = split_parts(shed)
    first = out[0].astype(F32) - jnp.where(place == 0, 1.0, 0.0) * shed
    last = out[rows - 1].astype(F32) + jnp.where(place == count - 1, 1.0, 0.0) * shed
    return out.at[0].set(first.astype(BF16)).at[rows - 1].set(last.astype(BF16))


def solution(mesh):
    in_specs = (
        P("chord", "span", None, None),
        P(None, "chord", "span", None, None),
        P(None, "chord", "span"),
        P("chord", "span", None, None, None, None),
        P("chord", "span", None),
        P(("span", "chord"), None, None),
        P(("span", "chord"), None),
        P(("span", "chord")),
    )
    out_specs = P("chord", "span", None, None)
    return jax.shard_map(
        per_device, mesh=mesh, in_specs=in_specs, out_specs=out_specs, check_vma=False
    )
```

```python
import jax
import jax.numpy as jnp
from jax import lax
from jax.experimental import pallas as pl
from jax.experimental.pallas import tpu as pltpu
from jax.sharding import PartitionSpec as P

BC = 8
BS = 16
R = 384
CAP = 32
LANES = 128
META = 192
ROWS = 208
F32 = jnp.float32
BF16 = jnp.bfloat16


def split_parts(array):
    return jnp.swapaxes(array, -3, -2)


def shift(array, axis, step):
    count = lax.axis_size(axis)
    pairs = [(i, i + step) for i in range(count) if 0 <= i + step < count]
    return lax.ppermute(array, axis, pairs)


def pack_kernel(owner_ref, station_ref, wake_ref, out_ref):
    rows = owner_ref.shape[1]
    owners = out_ref.shape[0]
    owner = owner_ref[...]
    station = station_ref[...]
    named = lax.broadcasted_iota(jnp.int32, (owners, rows), 0) == owner
    hot = jnp.where(named, 1.0, 0.0).astype(F32)
    before = jnp.where(
        lax.broadcasted_iota(jnp.int32, (rows, rows), 0)
        < lax.broadcasted_iota(jnp.int32, (rows, rows), 1),
        1.0,
        0.0,
    ).astype(BF16)
    counts = jnp.dot(hot.astype(BF16), before, preferred_element_type=F32)
    rank = jnp.sum(hot * counts, axis=0, keepdims=True).astype(jnp.int32)
    slot = owner * CAP + rank
    stations = jnp.where(named, (station + 1).astype(F32), 0.0).astype(BF16)
    ranks = jnp.where(
        lax.broadcasted_iota(jnp.int32, (LANES, rows), 0) == rank, 1.0, 0.0
    ).astype(BF16)
    meta = lax.dot_general(
        stations, ranks, (((1,), (1,)), ((), ())), preferred_element_type=F32
    ).astype(BF16)
    for d in range(owners):
        out_ref[d, META:ROWS, :] = jnp.broadcast_to(meta[d : d + 1], (ROWS - META, LANES))
    values = jnp.concatenate([wake_ref[0], wake_ref[1]], axis=1)
    chunk = 256
    for first in range(0, owners * CAP, chunk):
        place = jnp.where(
            lax.broadcasted_iota(jnp.int32, (chunk, rows), 0) + first == slot, 1.0, 0.0
        ).astype(BF16)
        packed = jnp.dot(place, values, preferred_element_type=F32).astype(BF16)
        for d in range(chunk // CAP):
            for part in range(6):
                out_ref[first // CAP + d, part * CAP : (part + 1) * CAP, :] = packed[
                    d * CAP : (d + 1) * CAP, part * LANES : (part + 1) * LANES
                ]


def pack(owner, station, wake, owners):
    return pl.pallas_call(
        pack_kernel,
        out_shape=jax.ShapeDtypeStruct((owners, ROWS, LANES), BF16),
        compiler_params=pltpu.CompilerParams(vmem_limit_bytes=32 * 1024 * 1024),
        name="wake_pack",
    )(owner, station, wake)


def sum_kernel(got_ref, out_ref):
    sources = got_ref.shape[0]
    width = out_ref.shape[1]
    group = LANES // CAP
    total = jnp.zeros((width, 6 * LANES), F32)
    for first in range(0, sources, 2 * group):
        hots, values = [], []
        for half in range(2):
            base = first + half * group
            codes = jnp.zeros((ROWS - META, LANES), F32)
            for q in range(group):
                row = got_ref[base + q, META:ROWS, :].astype(F32)
                codes = codes + (pltpu.roll(row, q * CAP, axis=1) if q else row)
            wanted = lax.broadcasted_iota(jnp.int32, (width, LANES), 0).astype(F32) + 1.0
            hots.append(jnp.where(codes[0:1] == wanted, 1.0, 0.0).astype(BF16))
            values.append(
                jnp.concatenate(
                    [
                        got_ref[base : base + group, part * CAP : (part + 1) * CAP, :].reshape(
                            LANES, LANES
                        )
                        for part in range(6)
                    ],
                    axis=1,
                )
            )
        total = total + jnp.dot(
            jnp.concatenate(hots, axis=1),
            jnp.concatenate(values, axis=0),
            preferred_element_type=F32,
        )
    out_ref[0] = total[:, :R]
    out_ref[1] = total[:, R:]


def sum_stations(got, width):
    return pl.pallas_call(
        sum_kernel,
        out_shape=jax.ShapeDtypeStruct((2, width, R), F32),
        compiler_params=pltpu.CompilerParams(vmem_limit_bytes=32 * 1024 * 1024),
        name="wake_sum",
    )(got)


def surface_kernel(
    inside,
    codes_ref,
    place_ref,
    own_ref,
    low_ref,
    high_ref,
    inner_ref,
    outer_ref,
    inner_corner_ref,
    outer_corner_ref,
    aic_ref,
    down_ref,
    before_ref,
    after_ref,
    along_ref,
    metric_ref,
    *rest,
):
    out_ref, blocks, factors, stage, weights, spread, gradient, rim, chord_row, mixed = rest[-10:]
    step = pl.program_id(0)
    c = pl.program_id(1)
    steps = pl.num_programs(0)
    t = target_row(inside, step)
    cols = own_ref.shape[2]
    brows = own_ref.shape[0] // BC
    bcols = cols // BS
    rows = metric_ref.shape[1]
    even = place_ref[0] == 0
    lane_sets = [slice(n * LANES, (n + 1) * LANES) for n in range(R // LANES)]

    @pl.when((step == 0) & (c == 0))
    def _():
        def put(r, q, source, row, col):
            for n, lanes in enumerate(lane_sets):
                for part in range(2):
                    for a in range(BC):
                        blocks[r, q, n, part, a * BS : (a + 1) * BS, :] = source[
                            row + a, part, col : col + BS, lanes
                        ]

        for q in range(bcols):
            for r in range(brows):
                put(r + 1, q + 1, own_ref, r * BC, q * BS)
            if not inside:
                put(0, q + 1, low_ref, 0, q * BS)
                put(brows + 1, q + 1, high_ref, 0, q * BS)
        if not inside:
            for n, lanes in enumerate(lane_sets):
                for part in range(2):
                    chord_row[0, n, part] = low_ref[BC, part, :, lanes]
                    chord_row[1, n, part] = high_ref[BC, part, :, lanes]

        def sides(left, right, left_corner, right_corner):
            for r in range(brows):
                put(r + 1, 0, left, r * BC, 0)
                put(r + 1, bcols + 1, right, r * BC, 0)
            if not inside:
                put(0, 0, left_corner, 0, 0)
                put(brows + 1, 0, left_corner, BC, 0)
                put(0, bcols + 1, right_corner, 0, 0)
                put(brows + 1, bcols + 1, right_corner, BC, 0)
            for piece in range(rows // BS):
                here = slice(piece * BS, (piece + 1) * BS)
                for n, lanes in enumerate(lane_sets):
                    for part in range(2):
                        rim[n, 0, part, here] = left[rows + piece, part, :, lanes].astype(F32)
                        rim[n, 1, part, here] = right[rows + piece, part, :, lanes].astype(F32)

        @pl.when(even)
        def _():
            sides(outer_ref, inner_ref, outer_corner_ref, inner_corner_ref)

        @pl.when(jnp.logical_not(even))
        def _():
            sides(inner_ref, outer_ref, inner_corner_ref, outer_corner_ref)

    @pl.when(c == 0)
    def _():
        diagonal = lax.broadcasted_iota(jnp.int32, (cols, cols), 0) == lax.broadcasted_iota(
            jnp.int32, (cols, cols), 1
        )
        for component in range(2):
            for a in range(component, BC + 2 - component):
                i = jnp.clip(t * BC - 1 + a, 0, rows - 1)
                line = metric_ref[component, pl.ds(i, 1), :]
                column = jnp.sum(jnp.where(diagonal, line, 0.0), axis=1, keepdims=True)
                factors[component, a] = jnp.broadcast_to(column, (cols, LANES))

    def weighted(ref, slot, factor):
        stage[slot] = ref.reshape(2 * cols, LANES)[...].astype(F32)
        return [stage[slot, pl.ds(part, cols, stride=2), :] * factor for part in range(2)]

    sources = [before_ref.at[0, 0]] + [down_ref.at[0, a] for a in range(BC)] + [after_ref.at[0, 0]]
    for a, source in enumerate(sources):
        pair = weighted(source, a, factors[0, a])
        for part in range(2):
            weights[a, part] = pair[part].astype(BF16)

    if not inside:

        @pl.when(step == 0)
        def _():
            weights[0] = chord_row[0, c]

        @pl.when(step == steps - 1)
        def _():
            weights[BC + 1] = chord_row[1, c]

    for a in range(BC):
        pair = weighted(along_ref.at[0, a], BC + 2 + a, factors[1, a + 1])
        for part in range(2):
            line = spread.at[a, part]
            line[8 : 8 + cols, :] = pair[part]
            line[7:8, :] = rim[c, 0, part, pl.ds(t * BC + a, 1), :]
            line[8 + cols : 9 + cols, :] = rim[c, 1, part, pl.ds(t * BC + a, 1), :]
            along = line[7 : 7 + cols, :] - line[9 : 9 + cols, :]
            down = weights[a, part].astype(F32) - weights[a + 2, part].astype(F32)
            gradient[a, part] = 0.5 * (down + along)

    for u in range(bcols):
        total = jnp.zeros((BC * BS, 2 * LANES), F32)
        for k in range(aic_ref.shape[2]):
            code = codes_ref[t, u, k]
            r = t + code // 3
            q = u + code % 3
            real = blocks[r, q, c, 0]
            imag = blocks[r, q, c, 1]
            source = jnp.concatenate(
                [
                    jnp.concatenate([real, imag], axis=1),
                    jnp.concatenate([-imag, real], axis=1),
                ],
                axis=0,
            )
            matrix = jnp.concatenate([aic_ref[0, u, k, 0], aic_ref[0, u, k, 1]], axis=1)
            total = total + jnp.dot(matrix, source, preferred_element_type=F32)
        for a in range(BC):
            for part in range(2):
                near = total[a * BS : (a + 1) * BS, part * LANES : (part + 1) * LANES]
                slope = gradient[a, part, u * BS : (u + 1) * BS, :]
                mixed[a, pl.ds(2 * u * BS + part, BS, stride=2), :] = near + slope
    for a in range(BC):
        out_ref.at[a].reshape(2 * cols, LANES)[...] = mixed[a].astype(BF16)


def target_row(inside, step):
    return step + 1 if inside else 3 * step


def surface(inside, codes, place, own, halos, aic, velocity, metric, done=None):
    rows, _, cols, _ = own.shape
    brows, bcols = rows // BC, cols // BS

    def whole(array):
        return pl.BlockSpec(array.shape, lambda s, c: (0,) * array.ndim)

    scalars = pl.BlockSpec(memory_space=pltpu.SMEM)
    line = (1, 1, cols, 2, LANES)
    strips = (1, BC, cols, 2, LANES)

    def row(s):
        return target_row(inside, s)

    def before(s, c):
        return (0, jnp.maximum(row(s) * BC - 1, 0), 0, 0, c)

    def after(s, c):
        return (0, jnp.minimum(row(s) * BC + BC, rows - 1), 0, 0, c)

    arguments = [codes, place, own, *halos, aic, velocity, velocity, velocity, velocity, metric]
    specs = (
        [scalars] * 2
        + [whole(array) for array in (own, *halos)]
        + [
            pl.BlockSpec((1,) + aic.shape[1:], lambda s, c: (row(s), 0, 0, 0, 0, 0)),
            pl.BlockSpec(strips, lambda s, c: (0, row(s), 0, 0, c)),
            pl.BlockSpec(line, before),
            pl.BlockSpec(line, after),
            pl.BlockSpec(strips, lambda s, c: (1, row(s), 0, 0, c)),
            whole(metric),
        ]
    )
    aliases = {}
    if done is not None:
        aliases = {len(arguments): 0}
        arguments.append(done)
        specs.append(pl.BlockSpec(memory_space=pl.ANY))

    def kernel(*refs):
        if inside:
            refs = refs[:3] + (None, None) + refs[3:5] + (None, None) + refs[5:]
        surface_kernel(inside, *refs)

    return pl.pallas_call(
        kernel,
        grid=(brows // 2, R // LANES),
        in_specs=specs,
        out_specs=pl.BlockSpec((BC, cols, 2, LANES), lambda s, c: (row(s), 0, 0, c)),
        out_shape=jax.ShapeDtypeStruct((rows, cols, 2, R), BF16),
        scratch_shapes=[
            pltpu.VMEM((brows + 2, bcols + 2, R // LANES, 2, BC * BS, LANES), BF16),
            pltpu.VMEM((2, BC + 2, cols, LANES), F32),
            pltpu.VMEM((2 * BC + 2, 2 * cols, LANES), F32),
            pltpu.VMEM((BC + 2, 2, cols, LANES), BF16),
            pltpu.VMEM((BC, 2, cols + 16, LANES), F32),
            pltpu.VMEM((BC, 2, cols, LANES), F32),
            pltpu.VMEM((R // LANES, 2, 2, rows, LANES), F32),
            pltpu.VMEM((2, R // LANES, 2, cols, LANES), BF16),
            pltpu.VMEM((BC, 2 * cols, LANES), F32),
        ],
        input_output_aliases=aliases,
        compiler_params=pltpu.CompilerParams(vmem_limit_bytes=56 * 1024 * 1024),
        cost_estimate=pl.CostEstimate(
            flops=3_250_000_000, bytes_accessed=14_000_000, transcendentals=0
        ),
        name="surface_inside" if inside else "surface_rim",
    )(*arguments)


def per_device(
    surface_adjoint,
    velocity_adjoint,
    metric,
    aic_blocks,
    block_codes,
    wake_adjoint,
    wake_owner,
    shed_station,
):
    rows, cols = surface_adjoint.shape[:2]
    owners = lax.axis_size("span")
    core = lax.axis_index("span") % 2
    own = split_parts(surface_adjoint)

    def weigh(factor, value):
        return (factor[..., None, None] * value.astype(F32)).astype(BF16)

    up_row = split_parts(weigh(metric[0, rows - 1], velocity_adjoint[0, rows - 1]))
    down_row = split_parts(weigh(metric[0, 0], velocity_adjoint[0, 0]))
    up_send = jnp.concatenate([own[rows - BC :], up_row[None]], axis=0)
    down_send = jnp.concatenate([own[:BC], down_row[None]], axis=0)
    inner_pairs = [(i, i ^ 1) for i in range(owners)]
    outer_pairs = [(i, i + 1) for i in range(1, owners - 1, 2)]
    outer_pairs = outer_pairs + [(j, i) for i, j in outer_pairs]
    inner_col = (1 - core) * (cols - BS)
    outer_col = core * (cols - BS)

    def side(first_col, lone_col):
        strip = lax.dynamic_slice_in_dim(own, first_col, BS, axis=2)
        lone = lax.dynamic_slice(velocity_adjoint, (1, 0, lone_col, 0, 0), (1, rows, 1, 2, R))
        lone = lone[0, :, 0]
        scale = lax.dynamic_slice(metric, (1, 0, lone_col), (1, rows, 1))[0, :, 0]
        lone = split_parts(weigh(scale, lone).reshape(rows // BS, BS, 2, R))
        return jnp.concatenate([strip, lone], axis=0)

    inner_send = side(inner_col, (1 - core) * (cols - 1))
    outer_send = side(outer_col, core * (cols - 1))
    inner = lax.ppermute(inner_send, "span", inner_pairs)
    outer = lax.ppermute(outer_send, "span", outer_pairs)
    up_send, down_send, wake = lax.optimization_barrier((up_send, down_send, wake_adjoint))
    low = shift(up_send, "chord", 1)
    high = shift(down_send, "chord", -1)

    packed = pack(
        wake_owner.reshape(1, -1), shed_station.reshape(1, -1), jnp.swapaxes(wake, 0, 1), owners
    )
    packed, inner, outer = lax.optimization_barrier((packed, inner, outer))
    got = lax.all_to_all(packed, "span", 0, 0, tiled=True)

    place = jnp.full((1,), core, jnp.int32)
    shared = (aic_blocks, velocity_adjoint, metric)
    out = surface(True, block_codes, place, own, (inner, outer), *shared)
    low, high, out = lax.optimization_barrier((low, high, out))

    def corner(first_col):
        return jnp.concatenate(
            [lax.dynamic_slice(ref, (0, 0, first_col, 0), (BC, 2, BS, R)) for ref in (low, high)],
            axis=0,
        )

    inner_corner = lax.ppermute(corner(inner_col), "span", inner_pairs)
    outer_corner = lax.ppermute(corner(outer_col), "span", outer_pairs)
    halos = (low, high, inner, outer, inner_corner, outer_corner)
    out = surface(False, block_codes, place, own, halos, *shared, done=out)

    partial = sum_stations(got, cols)
    count = lax.axis_size("chord")
    place = lax.axis_index("chord")
    half = count // 2
    pairs = [(i, 0 if i < half else count - 1) for i in (1, count - 2)]
    partial = partial + lax.ppermute(partial.astype(BF16), "chord", pairs).astype(F32)
    swap = [(0, count - 1), (count - 1, 0)]
    shed = partial + lax.ppermute(partial.astype(BF16), "chord", swap).astype(F32)
    shed = split_parts(shed)
    first = out[0].astype(F32) - jnp.where(place == 0, 1.0, 0.0) * shed
    last = out[rows - 1].astype(F32) + jnp.where(place == count - 1, 1.0, 0.0) * shed
    return out.at[0].set(first.astype(BF16)).at[rows - 1].set(last.astype(BF16))


def solution(mesh):
    in_specs = (
        P("chord", "span", None, None),
        P(None, "chord", "span", None, None),
        P(None, "chord", "span"),
        P("chord", "span", None, None, None, None),
        P("chord", "span", None),
        P(("span", "chord"), None, None),
        P(("span", "chord"), None),
        P(("span", "chord")),
    )
    out_specs = P("chord", "span", None, None)
    return jax.shard_map(
        per_device, mesh=mesh, in_specs=in_specs, out_specs=out_specs, check_vma=False
    )
```

```python
import jax
import jax.numpy as jnp
from jax import lax
from jax.experimental import pallas as pl
from jax.experimental.pallas import tpu as pltpu
from jax.sharding import PartitionSpec as P

BC = 8
BS = 16
R = 384
CAP = 32
LANES = 128
META = 192
ROWS = 208
F32 = jnp.float32
BF16 = jnp.bfloat16


def split_parts(array):
    return jnp.swapaxes(array, -3, -2)


def shift(array, axis, step):
    count = lax.axis_size(axis)
    pairs = [(i, i + step) for i in range(count) if 0 <= i + step < count]
    return lax.ppermute(array, axis, pairs)


def pack_kernel(owner_ref, station_ref, wake_ref, out_ref):
    rows = owner_ref.shape[1]
    owners = out_ref.shape[0]
    owner = owner_ref[...]
    station = station_ref[...]
    named = lax.broadcasted_iota(jnp.int32, (owners, rows), 0) == owner
    hot = jnp.where(named, 1.0, 0.0).astype(F32)
    before = jnp.where(
        lax.broadcasted_iota(jnp.int32, (rows, rows), 0)
        < lax.broadcasted_iota(jnp.int32, (rows, rows), 1),
        1.0,
        0.0,
    ).astype(BF16)
    counts = jnp.dot(hot.astype(BF16), before, preferred_element_type=F32)
    rank = jnp.sum(hot * counts, axis=0, keepdims=True).astype(jnp.int32)
    slot = owner * CAP + rank
    stations = jnp.where(named, (station + 1).astype(F32), 0.0).astype(BF16)
    ranks = jnp.where(
        lax.broadcasted_iota(jnp.int32, (LANES, rows), 0) == rank, 1.0, 0.0
    ).astype(BF16)
    meta = lax.dot_general(
        stations, ranks, (((1,), (1,)), ((), ())), preferred_element_type=F32
    ).astype(BF16)
    for d in range(owners):
        out_ref[d, META:ROWS, :] = jnp.broadcast_to(meta[d : d + 1], (ROWS - META, LANES))
    values = jnp.concatenate([wake_ref[0], wake_ref[1]], axis=1)
    chunk = 256
    for first in range(0, owners * CAP, chunk):
        place = jnp.where(
            lax.broadcasted_iota(jnp.int32, (chunk, rows), 0) + first == slot, 1.0, 0.0
        ).astype(BF16)
        packed = jnp.dot(place, values, preferred_element_type=F32).astype(BF16)
        for d in range(chunk // CAP):
            for part in range(6):
                out_ref[first // CAP + d, part * CAP : (part + 1) * CAP, :] = packed[
                    d * CAP : (d + 1) * CAP, part * LANES : (part + 1) * LANES
                ]


def pack(owner, station, wake, owners):
    return pl.pallas_call(
        pack_kernel,
        out_shape=jax.ShapeDtypeStruct((owners, ROWS, LANES), BF16),
        compiler_params=pltpu.CompilerParams(vmem_limit_bytes=32 * 1024 * 1024),
        name="wake_pack",
    )(owner, station, wake)


def sum_kernel(got_ref, out_ref):
    sources = got_ref.shape[0]
    width = out_ref.shape[1]
    group = LANES // CAP
    total = jnp.zeros((width, 6 * LANES), F32)
    for first in range(0, sources, 2 * group):
        hots, values = [], []
        for half in range(2):
            base = first + half * group
            codes = jnp.zeros((ROWS - META, LANES), F32)
            for q in range(group):
                row = got_ref[base + q, META:ROWS, :].astype(F32)
                codes = codes + (pltpu.roll(row, q * CAP, axis=1) if q else row)
            wanted = lax.broadcasted_iota(jnp.int32, (width, LANES), 0).astype(F32) + 1.0
            hots.append(jnp.where(codes[0:1] == wanted, 1.0, 0.0).astype(BF16))
            values.append(
                jnp.concatenate(
                    [
                        got_ref[base : base + group, part * CAP : (part + 1) * CAP, :].reshape(
                            LANES, LANES
                        )
                        for part in range(6)
                    ],
                    axis=1,
                )
            )
        total = total + jnp.dot(
            jnp.concatenate(hots, axis=1),
            jnp.concatenate(values, axis=0),
            preferred_element_type=F32,
        )
    out_ref[0] = total[:, :R]
    out_ref[1] = total[:, R:]


def sum_stations(got, width):
    return pl.pallas_call(
        sum_kernel,
        out_shape=jax.ShapeDtypeStruct((2, width, R), F32),
        compiler_params=pltpu.CompilerParams(vmem_limit_bytes=32 * 1024 * 1024),
        name="wake_sum",
    )(got)


def surface_kernel(
    inside,
    codes_ref,
    place_ref,
    own_ref,
    low_ref,
    high_ref,
    inner_ref,
    outer_ref,
    inner_corner_ref,
    outer_corner_ref,
    aic_ref,
    down_ref,
    before_ref,
    after_ref,
    along_ref,
    metric_ref,
    *rest,
):
    out_ref, blocks, factors, stage, weights, spread, gradient, rim, chord_row, mixed, near = (
        rest[-11:]
    )
    step = pl.program_id(0)
    c = pl.program_id(1)
    steps = pl.num_programs(0)
    t = target_row(inside, step)
    cols = own_ref.shape[2]
    brows = own_ref.shape[0] // BC
    bcols = cols // BS
    rows = metric_ref.shape[1]
    even = place_ref[0] == 0
    lane_sets = [slice(n * LANES, (n + 1) * LANES) for n in range(R // LANES)]

    @pl.when((step == 0) & (c == 0))
    def _():
        def put(r, q, source, row, col):
            for n, lanes in enumerate(lane_sets):
                for part in range(2):
                    for a in range(BC):
                        blocks[r, q, n, part, a * BS : (a + 1) * BS, :] = source[
                            row + a, part, col : col + BS, lanes
                        ]

        for q in range(bcols):
            for r in range(brows):
                put(r + 1, q + 1, own_ref, r * BC, q * BS)
            if not inside:
                put(0, q + 1, low_ref, 0, q * BS)
                put(brows + 1, q + 1, high_ref, 0, q * BS)
        if not inside:
            for n, lanes in enumerate(lane_sets):
                for part in range(2):
                    chord_row[0, n, part] = low_ref[BC, part, :, lanes]
                    chord_row[1, n, part] = high_ref[BC, part, :, lanes]

        def sides(left, right, left_corner, right_corner):
            for r in range(brows):
                put(r + 1, 0, left, r * BC, 0)
                put(r + 1, bcols + 1, right, r * BC, 0)
            if not inside:
                put(0, 0, left_corner, 0, 0)
                put(brows + 1, 0, left_corner, BC, 0)
                put(0, bcols + 1, right_corner, 0, 0)
                put(brows + 1, bcols + 1, right_corner, BC, 0)
            for piece in range(rows // BS):
                here = slice(piece * BS, (piece + 1) * BS)
                for n, lanes in enumerate(lane_sets):
                    for part in range(2):
                        rim[n, 0, part, here] = left[rows + piece, part, :, lanes].astype(F32)
                        rim[n, 1, part, here] = right[rows + piece, part, :, lanes].astype(F32)

        @pl.when(even)
        def _():
            sides(outer_ref, inner_ref, outer_corner_ref, inner_corner_ref)

        @pl.when(jnp.logical_not(even))
        def _():
            sides(inner_ref, outer_ref, inner_corner_ref, outer_corner_ref)

    @pl.when(c == 0)
    def _():
        diagonal = lax.broadcasted_iota(jnp.int32, (cols, cols), 0) == lax.broadcasted_iota(
            jnp.int32, (cols, cols), 1
        )
        for component in range(2):
            for a in range(component, BC + 2 - component):
                i = jnp.clip(t * BC - 1 + a, 0, rows - 1)
                line = metric_ref[component, pl.ds(i, 1), :]
                column = jnp.sum(jnp.where(diagonal, line, 0.0), axis=1, keepdims=True)
                factors[component, a] = jnp.broadcast_to(column, (cols, LANES))

    def weighted(ref, slot, factor):
        stage[slot] = ref.reshape(2 * cols, LANES)[...].astype(F32)
        return [stage[slot, pl.ds(part, cols, stride=2), :] * factor for part in range(2)]

    sources = [before_ref.at[0, 0]] + [down_ref.at[0, a] for a in range(BC)] + [after_ref.at[0, 0]]
    def weigh_row(a):
        pair = weighted(sources[a], a, factors[0, a])
        for part in range(2):
            value = pair[part].astype(BF16)
            if not inside and a == 0:
                value = jnp.where(step == 0, chord_row[0, c, part], value)
            if not inside and a == BC + 1:
                value = jnp.where(step == steps - 1, chord_row[1, c, part], value)
            weights[a, part] = value

    def slope_row(a):
        pair = weighted(along_ref.at[0, a], BC + 2 + a, factors[1, a + 1])
        for part in range(2):
            line = spread.at[a, part]
            line[8 : 8 + cols, :] = pair[part]
            line[7:8, :] = rim[c, 0, part, pl.ds(t * BC + a, 1), :]
            line[8 + cols : 9 + cols, :] = rim[c, 1, part, pl.ds(t * BC + a, 1), :]
            along = line[7 : 7 + cols, :] - line[9 : 9 + cols, :]
            down = weights[a, part].astype(F32) - weights[a + 2, part].astype(F32)
            gradient[a, part] = 0.5 * (down + along)

    work = [(weigh_row, a) for a in range(3)]
    for a in range(BC):
        work.append((slope_row, a))
        if a + 3 < BC + 2:
            work.append((weigh_row, a + 3))
    slots = aic_ref.shape[2]
    turns = bcols * slots
    for u in range(bcols):
        total = jnp.zeros((BC * BS, 2 * LANES), F32)
        for k in range(slots):
            turn = u * slots + k
            for call, a in work[turn * len(work) // turns : (turn + 1) * len(work) // turns]:
                call(a)
            code = codes_ref[t, u, k]
            r = t + code // 3
            q = u + code % 3
            real = blocks[r, q, c, 0]
            imag = blocks[r, q, c, 1]
            source = jnp.concatenate(
                [
                    jnp.concatenate([real, imag], axis=1),
                    jnp.concatenate([-imag, real], axis=1),
                ],
                axis=0,
            )
            matrix = jnp.concatenate([aic_ref[0, u, k, 0], aic_ref[0, u, k, 1]], axis=1)
            total = total + jnp.dot(matrix, source, preferred_element_type=F32)
        near[u] = total
    for a in range(BC):
        for u in range(bcols):
            for part in range(2):
                value = near[u, a * BS : (a + 1) * BS, part * LANES : (part + 1) * LANES]
                slope = gradient[a, part, u * BS : (u + 1) * BS, :]
                mixed[a, pl.ds(2 * u * BS + part, BS, stride=2), :] = value + slope
        out_ref.at[a].reshape(2 * cols, LANES)[...] = mixed[a].astype(BF16)


def target_row(inside, step):
    return step + 1 if inside else 3 * step


def surface(inside, codes, place, own, halos, aic, velocity, metric, done=None):
    rows, _, cols, _ = own.shape
    brows, bcols = rows // BC, cols // BS

    def whole(array):
        return pl.BlockSpec(array.shape, lambda s, c: (0,) * array.ndim)

    scalars = pl.BlockSpec(memory_space=pltpu.SMEM)
    line = (1, 1, cols, 2, LANES)
    strips = (1, BC, cols, 2, LANES)

    def row(s):
        return target_row(inside, s)

    def before(s, c):
        return (0, jnp.maximum(row(s) * BC - 1, 0), 0, 0, c)

    def after(s, c):
        return (0, jnp.minimum(row(s) * BC + BC, rows - 1), 0, 0, c)

    arguments = [codes, place, own, *halos, aic, velocity, velocity, velocity, velocity, metric]
    specs = (
        [scalars] * 2
        + [whole(array) for array in (own, *halos)]
        + [
            pl.BlockSpec((1,) + aic.shape[1:], lambda s, c: (row(s), 0, 0, 0, 0, 0)),
            pl.BlockSpec(strips, lambda s, c: (0, row(s), 0, 0, c)),
            pl.BlockSpec(line, before),
            pl.BlockSpec(line, after),
            pl.BlockSpec(strips, lambda s, c: (1, row(s), 0, 0, c)),
            whole(metric),
        ]
    )
    aliases = {}
    if done is not None:
        aliases = {len(arguments): 0}
        arguments.append(done)
        specs.append(pl.BlockSpec(memory_space=pl.ANY))

    def kernel(*refs):
        if inside:
            refs = refs[:3] + (None, None) + refs[3:5] + (None, None) + refs[5:]
        surface_kernel(inside, *refs)

    return pl.pallas_call(
        kernel,
        grid=(brows // 2, R // LANES),
        in_specs=specs,
        out_specs=pl.BlockSpec((BC, cols, 2, LANES), lambda s, c: (row(s), 0, 0, c)),
        out_shape=jax.ShapeDtypeStruct((rows, cols, 2, R), BF16),
        scratch_shapes=[
            pltpu.VMEM((brows + 2, bcols + 2, R // LANES, 2, BC * BS, LANES), BF16),
            pltpu.VMEM((2, BC + 2, cols, LANES), F32),
            pltpu.VMEM((2 * BC + 2, 2 * cols, LANES), F32),
            pltpu.VMEM((BC + 2, 2, cols, LANES), BF16),
            pltpu.VMEM((BC, 2, cols + 16, LANES), F32),
            pltpu.VMEM((BC, 2, cols, LANES), F32),
            pltpu.VMEM((R // LANES, 2, 2, rows, LANES), F32),
            pltpu.VMEM((2, R // LANES, 2, cols, LANES), BF16),
            pltpu.VMEM((BC, 2 * cols, LANES), F32),
            pltpu.VMEM((bcols, BC * BS, 2 * LANES), F32),
        ],
        input_output_aliases=aliases,
        compiler_params=pltpu.CompilerParams(vmem_limit_bytes=56 * 1024 * 1024),
        cost_estimate=pl.CostEstimate(
            flops=3_250_000_000, bytes_accessed=14_000_000, transcendentals=0
        ),
        name="surface_inside" if inside else "surface_rim",
    )(*arguments)


def per_device(
    surface_adjoint,
    velocity_adjoint,
    metric,
    aic_blocks,
    block_codes,
    wake_adjoint,
    wake_owner,
    shed_station,
):
    rows, cols = surface_adjoint.shape[:2]
    owners = lax.axis_size("span")
    core = lax.axis_index("span") % 2
    own = split_parts(surface_adjoint)

    def weigh(factor, value):
        return (factor[..., None, None] * value.astype(F32)).astype(BF16)

    up_row = split_parts(weigh(metric[0, rows - 1], velocity_adjoint[0, rows - 1]))
    down_row = split_parts(weigh(metric[0, 0], velocity_adjoint[0, 0]))
    up_send = jnp.concatenate([own[rows - BC :], up_row[None]], axis=0)
    down_send = jnp.concatenate([own[:BC], down_row[None]], axis=0)
    inner_pairs = [(i, i ^ 1) for i in range(owners)]
    outer_pairs = [(i, i + 1) for i in range(1, owners - 1, 2)]
    outer_pairs = outer_pairs + [(j, i) for i, j in outer_pairs]
    inner_col = (1 - core) * (cols - BS)
    outer_col = core * (cols - BS)

    def side(first_col, lone_col):
        strip = lax.dynamic_slice_in_dim(own, first_col, BS, axis=2)
        lone = lax.dynamic_slice(velocity_adjoint, (1, 0, lone_col, 0, 0), (1, rows, 1, 2, R))
        lone = lone[0, :, 0]
        scale = lax.dynamic_slice(metric, (1, 0, lone_col), (1, rows, 1))[0, :, 0]
        lone = split_parts(weigh(scale, lone).reshape(rows // BS, BS, 2, R))
        return jnp.concatenate([strip, lone], axis=0)

    inner_send = side(inner_col, (1 - core) * (cols - 1))
    outer_send = side(outer_col, core * (cols - 1))
    inner = lax.ppermute(inner_send, "span", inner_pairs)
    outer = lax.ppermute(outer_send, "span", outer_pairs)
    up_send, down_send, wake = lax.optimization_barrier((up_send, down_send, wake_adjoint))
    low = shift(up_send, "chord", 1)
    high = shift(down_send, "chord", -1)

    packed = pack(
        wake_owner.reshape(1, -1), shed_station.reshape(1, -1), jnp.swapaxes(wake, 0, 1), owners
    )
    packed, inner, outer = lax.optimization_barrier((packed, inner, outer))
    got = lax.all_to_all(packed, "span", 0, 0, tiled=True)

    place = jnp.full((1,), core, jnp.int32)
    shared = (aic_blocks, velocity_adjoint, metric)
    out = surface(True, block_codes, place, own, (inner, outer), *shared)
    low, high, out = lax.optimization_barrier((low, high, out))

    def corner(first_col):
        return jnp.concatenate(
            [lax.dynamic_slice(ref, (0, 0, first_col, 0), (BC, 2, BS, R)) for ref in (low, high)],
            axis=0,
        )

    inner_corner = lax.ppermute(corner(inner_col), "span", inner_pairs)
    outer_corner = lax.ppermute(corner(outer_col), "span", outer_pairs)
    halos = (low, high, inner, outer, inner_corner, outer_corner)
    out = surface(False, block_codes, place, own, halos, *shared, done=out)

    partial = sum_stations(got, cols)
    count = lax.axis_size("chord")
    place = lax.axis_index("chord")
    half = count // 2
    pairs = [(i, 0 if i < half else count - 1) for i in (1, count - 2)]
    partial = partial + lax.ppermute(partial.astype(BF16), "chord", pairs).astype(F32)
    swap = [(0, count - 1), (count - 1, 0)]
    shed = partial + lax.ppermute(partial.astype(BF16), "chord", swap).astype(F32)
    shed = split_parts(shed)
    first = out[0].astype(F32) - jnp.where(place == 0, 1.0, 0.0) * shed
    last = out[rows - 1].astype(F32) + jnp.where(place == count - 1, 1.0, 0.0) * shed
    return out.at[0].set(first.astype(BF16)).at[rows - 1].set(last.astype(BF16))


def solution(mesh):
    in_specs = (
        P("chord", "span", None, None),
        P(None, "chord", "span", None, None),
        P(None, "chord", "span"),
        P("chord", "span", None, None, None, None),
        P("chord", "span", None),
        P(("span", "chord"), None, None),
        P(("span", "chord"), None),
        P(("span", "chord")),
    )
    out_specs = P("chord", "span", None, None)
    return jax.shard_map(
        per_device, mesh=mesh, in_specs=in_specs, out_specs=out_specs, check_vma=False
    )
```

```python
import jax
import jax.numpy as jnp
from jax import lax
from jax.experimental import pallas as pl
from jax.experimental.pallas import tpu as pltpu
from jax.sharding import PartitionSpec as P

BC = 8
BS = 16
R = 384
CAP = 32
LANES = 128
META = 192
ROWS = 208
F32 = jnp.float32
BF16 = jnp.bfloat16


def split_parts(array):
    return jnp.swapaxes(array, -3, -2)


def shift(array, axis, step):
    count = lax.axis_size(axis)
    pairs = [(i, i + step) for i in range(count) if 0 <= i + step < count]
    return lax.ppermute(array, axis, pairs)


def pack_kernel(owner_ref, station_ref, wake_ref, out_ref):
    rows = owner_ref.shape[1]
    owners = out_ref.shape[0]
    owner = owner_ref[...]
    station = station_ref[...]
    named = lax.broadcasted_iota(jnp.int32, (owners, rows), 0) == owner
    hot = jnp.where(named, 1.0, 0.0).astype(F32)
    before = jnp.where(
        lax.broadcasted_iota(jnp.int32, (rows, rows), 0)
        < lax.broadcasted_iota(jnp.int32, (rows, rows), 1),
        1.0,
        0.0,
    ).astype(BF16)
    counts = jnp.dot(hot.astype(BF16), before, preferred_element_type=F32)
    rank = jnp.sum(hot * counts, axis=0, keepdims=True).astype(jnp.int32)
    slot = owner * CAP + rank
    stations = jnp.where(named, (station + 1).astype(F32), 0.0).astype(BF16)
    ranks = jnp.where(
        lax.broadcasted_iota(jnp.int32, (LANES, rows), 0) == rank, 1.0, 0.0
    ).astype(BF16)
    meta = lax.dot_general(
        stations, ranks, (((1,), (1,)), ((), ())), preferred_element_type=F32
    ).astype(BF16)
    for d in range(owners):
        out_ref[d, META:ROWS, :] = jnp.broadcast_to(meta[d : d + 1], (ROWS - META, LANES))
    values = jnp.concatenate([wake_ref[0], wake_ref[1]], axis=1)
    chunk = 256
    for first in range(0, owners * CAP, chunk):
        place = jnp.where(
            lax.broadcasted_iota(jnp.int32, (chunk, rows), 0) + first == slot, 1.0, 0.0
        ).astype(BF16)
        packed = jnp.dot(place, values, preferred_element_type=F32).astype(BF16)
        for d in range(chunk // CAP):
            for part in range(6):
                out_ref[first // CAP + d, part * CAP : (part + 1) * CAP, :] = packed[
                    d * CAP : (d + 1) * CAP, part * LANES : (part + 1) * LANES
                ]


def pack(owner, station, wake, owners):
    return pl.pallas_call(
        pack_kernel,
        out_shape=jax.ShapeDtypeStruct((owners, ROWS, LANES), BF16),
        compiler_params=pltpu.CompilerParams(vmem_limit_bytes=32 * 1024 * 1024),
        name="wake_pack",
    )(owner, station, wake)


def sum_kernel(got_ref, out_ref):
    sources = got_ref.shape[0]
    width = out_ref.shape[1]
    group = LANES // CAP
    total = jnp.zeros((width, 6 * LANES), F32)
    for first in range(0, sources, 2 * group):
        hots, values = [], []
        for half in range(2):
            base = first + half * group
            codes = jnp.zeros((ROWS - META, LANES), F32)
            for q in range(group):
                row = got_ref[base + q, META:ROWS, :].astype(F32)
                codes = codes + (pltpu.roll(row, q * CAP, axis=1) if q else row)
            wanted = lax.broadcasted_iota(jnp.int32, (width, LANES), 0).astype(F32) + 1.0
            hots.append(jnp.where(codes[0:1] == wanted, 1.0, 0.0).astype(BF16))
            values.append(
                jnp.concatenate(
                    [
                        got_ref[base : base + group, part * CAP : (part + 1) * CAP, :].reshape(
                            LANES, LANES
                        )
                        for part in range(6)
                    ],
                    axis=1,
                )
            )
        total = total + jnp.dot(
            jnp.concatenate(hots, axis=1),
            jnp.concatenate(values, axis=0),
            preferred_element_type=F32,
        )
    out_ref[0] = total[:, :R]
    out_ref[1] = total[:, R:]


def sum_stations(got, width):
    return pl.pallas_call(
        sum_kernel,
        out_shape=jax.ShapeDtypeStruct((2, width, R), F32),
        compiler_params=pltpu.CompilerParams(vmem_limit_bytes=32 * 1024 * 1024),
        name="wake_sum",
    )(got)


def surface_kernel(
    inside,
    codes_ref,
    place_ref,
    own_ref,
    low_ref,
    high_ref,
    inner_ref,
    outer_ref,
    inner_corner_ref,
    outer_corner_ref,
    aic_ref,
    down_ref,
    before_ref,
    after_ref,
    along_ref,
    metric_ref,
    *rest,
):
    out_ref, blocks, factors, stage, weights, spread, gradient, rim, chord_row, mixed, near = (
        rest[-11:]
    )
    step = pl.program_id(0)
    c = pl.program_id(1)
    steps = pl.num_programs(0)
    t = target_row(inside, step)
    cols = own_ref.shape[2]
    brows = own_ref.shape[0] // BC
    bcols = cols // BS
    rows = metric_ref.shape[1]
    even = place_ref[0] == 0
    lane_sets = [slice(n * LANES, (n + 1) * LANES) for n in range(R // LANES)]

    @pl.when((step == 0) & (c == 0))
    def _():
        def put(r, q, source, row, col):
            for n, lanes in enumerate(lane_sets):
                for part in range(2):
                    for a in range(BC):
                        blocks[r, q, n, part, a * BS : (a + 1) * BS, :] = source[
                            row + a, part, col : col + BS, lanes
                        ]

        for q in range(bcols):
            for r in range(brows):
                put(r + 1, q + 1, own_ref, r * BC, q * BS)
            if not inside:
                put(0, q + 1, low_ref, 0, q * BS)
                put(brows + 1, q + 1, high_ref, 0, q * BS)
        if not inside:
            for n, lanes in enumerate(lane_sets):
                for part in range(2):
                    chord_row[0, n, part] = low_ref[BC, part, :, lanes]
                    chord_row[1, n, part] = high_ref[BC, part, :, lanes]

        def sides(left, right, left_corner, right_corner):
            for r in range(brows):
                put(r + 1, 0, left, r * BC, 0)
                put(r + 1, bcols + 1, right, r * BC, 0)
            if not inside:
                put(0, 0, left_corner, 0, 0)
                put(brows + 1, 0, left_corner, BC, 0)
                put(0, bcols + 1, right_corner, 0, 0)
                put(brows + 1, bcols + 1, right_corner, BC, 0)
            for piece in range(rows // BS):
                here = slice(piece * BS, (piece + 1) * BS)
                for n, lanes in enumerate(lane_sets):
                    for part in range(2):
                        rim[n, 0, part, here] = left[rows + piece, part, :, lanes].astype(F32)
                        rim[n, 1, part, here] = right[rows + piece, part, :, lanes].astype(F32)

        @pl.when(even)
        def _():
            sides(outer_ref, inner_ref, outer_corner_ref, inner_corner_ref)

        @pl.when(jnp.logical_not(even))
        def _():
            sides(inner_ref, outer_ref, inner_corner_ref, outer_corner_ref)

    @pl.when(c == 0)
    def _():
        diagonal = lax.broadcasted_iota(jnp.int32, (cols, cols), 0) == lax.broadcasted_iota(
            jnp.int32, (cols, cols), 1
        )
        for component in range(2):
            for a in range(component, BC + 2 - component):
                i = jnp.clip(t * BC - 1 + a, 0, rows - 1)
                line = metric_ref[component, pl.ds(i, 1), :]
                column = jnp.sum(jnp.where(diagonal, line, 0.0), axis=1, keepdims=True)
                factors[component, a] = jnp.broadcast_to(column, (cols, LANES))

    def weighted(ref, slot, factor):
        stage[slot] = ref.reshape(2 * cols, LANES)[...].astype(F32)
        return [stage[slot, pl.ds(part, cols, stride=2), :] * factor for part in range(2)]

    sources = [before_ref.at[0, 0]] + [down_ref.at[0, a] for a in range(BC)] + [after_ref.at[0, 0]]
    def weigh_row(a):
        pair = weighted(sources[a], a, factors[0, a])
        for part in range(2):
            value = pair[part].astype(BF16)
            if not inside and a == 0:
                value = jnp.where(step == 0, chord_row[0, c, part], value)
            if not inside and a == BC + 1:
                value = jnp.where(step == steps - 1, chord_row[1, c, part], value)
            weights[a, part] = value

    def slope_row(a):
        pair = weighted(along_ref.at[0, a], BC + 2 + a, factors[1, a + 1])
        for part in range(2):
            line = spread.at[a, part]
            line[8 : 8 + cols, :] = pair[part]
            line[7:8, :] = rim[c, 0, part, pl.ds(t * BC + a, 1), :]
            line[8 + cols : 9 + cols, :] = rim[c, 1, part, pl.ds(t * BC + a, 1), :]
            along = line[7 : 7 + cols, :] - line[9 : 9 + cols, :]
            down = weights[a, part].astype(F32) - weights[a + 2, part].astype(F32)
            gradient[a, part] = 0.5 * (down + along)

    work = [(weigh_row, a) for a in range(3)]
    for a in range(BC):
        work.append((slope_row, a))
        if a + 3 < BC + 2:
            work.append((weigh_row, a + 3))
    slots = aic_ref.shape[2]
    turns = bcols * slots
    for u in range(bcols):
        total = jnp.zeros((BC * BS, 2 * LANES), F32)
        for k in range(slots):
            turn = u * slots + k
            for call, a in work[turn * len(work) // turns : (turn + 1) * len(work) // turns]:
                call(a)
            code = codes_ref[t, u, k]
            r = t + code // 3
            q = u + code % 3
            real = blocks[r, q, c, 0]
            imag = blocks[r, q, c, 1]
            source = jnp.concatenate(
                [
                    jnp.concatenate([real, imag], axis=1),
                    jnp.concatenate([-imag, real], axis=1),
                ],
                axis=0,
            )
            matrix = jnp.concatenate([aic_ref[0, u, k, 0], aic_ref[0, u, k, 1]], axis=1)
            total = total + jnp.dot(matrix, source, preferred_element_type=F32)
        near[u] = total
    for a in range(BC):
        for u in range(bcols):
            for part in range(2):
                value = near[u, a * BS : (a + 1) * BS, part * LANES : (part + 1) * LANES]
                slope = gradient[a, part, u * BS : (u + 1) * BS, :]
                mixed[a, pl.ds(2 * u * BS + part, BS, stride=2), :] = value + slope
        out_ref.at[a].reshape(2 * cols, LANES)[...] = mixed[a].astype(BF16)


def target_row(inside, step):
    return step + 1 if inside else 3 * step


def surface(inside, codes, place, own, halos, aic, velocity, metric, done=None):
    rows, _, cols, _ = own.shape
    brows, bcols = rows // BC, cols // BS

    def whole(array):
        return pl.BlockSpec(array.shape, lambda s, c: (0,) * array.ndim)

    scalars = pl.BlockSpec(memory_space=pltpu.SMEM)
    line = (1, 1, cols, 2, LANES)
    strips = (1, BC, cols, 2, LANES)

    def row(s):
        return target_row(inside, s)

    def before(s, c):
        return (0, jnp.maximum(row(s) * BC - 1, 0), 0, 0, c)

    def after(s, c):
        return (0, jnp.minimum(row(s) * BC + BC, rows - 1), 0, 0, c)

    arguments = [codes, place, own, *halos, aic, velocity, velocity, velocity, velocity, metric]
    specs = (
        [scalars] * 2
        + [whole(array) for array in (own, *halos)]
        + [
            pl.BlockSpec((1,) + aic.shape[1:], lambda s, c: (row(s), 0, 0, 0, 0, 0)),
            pl.BlockSpec(strips, lambda s, c: (0, row(s), 0, 0, c)),
            pl.BlockSpec(line, before),
            pl.BlockSpec(line, after),
            pl.BlockSpec(strips, lambda s, c: (1, row(s), 0, 0, c)),
            whole(metric),
        ]
    )
    aliases = {}
    if done is not None:
        aliases = {len(arguments): 0}
        arguments.append(done)
        specs.append(pl.BlockSpec(memory_space=pl.ANY))

    def kernel(*refs):
        if inside:
            refs = refs[:3] + (None, None) + refs[3:5] + (None, None) + refs[5:]
        surface_kernel(inside, *refs)

    return pl.pallas_call(
        kernel,
        grid=(brows // 2, R // LANES),
        in_specs=specs,
        out_specs=pl.BlockSpec((BC, cols, 2, LANES), lambda s, c: (row(s), 0, 0, c)),
        out_shape=jax.ShapeDtypeStruct((rows, cols, 2, R), BF16),
        scratch_shapes=[
            pltpu.VMEM((brows + 2, bcols + 2, R // LANES, 2, BC * BS, LANES), BF16),
            pltpu.VMEM((2, BC + 2, cols, LANES), F32),
            pltpu.VMEM((2 * BC + 2, 2 * cols, LANES), F32),
            pltpu.VMEM((BC + 2, 2, cols, LANES), BF16),
            pltpu.VMEM((BC, 2, cols + 16, LANES), F32),
            pltpu.VMEM((BC, 2, cols, LANES), F32),
            pltpu.VMEM((R // LANES, 2, 2, rows, LANES), F32),
            pltpu.VMEM((2, R // LANES, 2, cols, LANES), BF16),
            pltpu.VMEM((BC, 2 * cols, LANES), F32),
            pltpu.VMEM((bcols, BC * BS, 2 * LANES), F32),
        ],
        input_output_aliases=aliases,
        compiler_params=pltpu.CompilerParams(vmem_limit_bytes=56 * 1024 * 1024),
        cost_estimate=pl.CostEstimate(
            flops=3_250_000_000, bytes_accessed=14_000_000, transcendentals=0
        ),
        name="surface_inside" if inside else "surface_rim",
    )(*arguments)


def per_device(
    surface_adjoint,
    velocity_adjoint,
    metric,
    aic_blocks,
    block_codes,
    wake_adjoint,
    wake_owner,
    shed_station,
):
    rows, cols = surface_adjoint.shape[:2]
    owners = lax.axis_size("span")
    core = lax.axis_index("span") % 2
    own = split_parts(surface_adjoint)

    def weigh(factor, value):
        return (factor[..., None, None] * value.astype(F32)).astype(BF16)

    up_row = split_parts(weigh(metric[0, rows - 1], velocity_adjoint[0, rows - 1]))
    down_row = split_parts(weigh(metric[0, 0], velocity_adjoint[0, 0]))
    up_send = jnp.concatenate([own[rows - BC :], up_row[None]], axis=0)
    down_send = jnp.concatenate([own[:BC], down_row[None]], axis=0)
    inner_pairs = [(i, i ^ 1) for i in range(owners)]
    outer_pairs = [(i, i + 1) for i in range(1, owners - 1, 2)]
    outer_pairs = outer_pairs + [(j, i) for i, j in outer_pairs]
    inner_col = (1 - core) * (cols - BS)
    outer_col = core * (cols - BS)

    def side(first_col, lone_col):
        strip = lax.dynamic_slice_in_dim(own, first_col, BS, axis=2)
        lone = lax.dynamic_slice(velocity_adjoint, (1, 0, lone_col, 0, 0), (1, rows, 1, 2, R))
        lone = lone[0, :, 0]
        scale = lax.dynamic_slice(metric, (1, 0, lone_col), (1, rows, 1))[0, :, 0]
        lone = split_parts(weigh(scale, lone).reshape(rows // BS, BS, 2, R))
        return jnp.concatenate([strip, lone], axis=0)

    inner_send = side(inner_col, (1 - core) * (cols - 1))
    outer_send = side(outer_col, core * (cols - 1))
    inner = lax.ppermute(inner_send, "span", inner_pairs)
    outer = lax.ppermute(outer_send, "span", outer_pairs)
    up_send, down_send, wake = lax.optimization_barrier((up_send, down_send, wake_adjoint))
    low = shift(up_send, "chord", 1)
    high = shift(down_send, "chord", -1)

    packed = pack(
        wake_owner.reshape(1, -1), shed_station.reshape(1, -1), jnp.swapaxes(wake, 0, 1), owners
    )
    packed, inner, outer = lax.optimization_barrier((packed, inner, outer))
    got = lax.all_to_all(packed, "span", 0, 0, tiled=True)

    place = jnp.full((1,), core, jnp.int32)
    shared = (aic_blocks, velocity_adjoint, metric)
    out = surface(True, block_codes, place, own, (inner, outer), *shared)
    low, high, out = lax.optimization_barrier((low, high, out))

    def corner(first_col):
        return jnp.concatenate(
            [lax.dynamic_slice(ref, (0, 0, first_col, 0), (BC, 2, BS, R)) for ref in (low, high)],
            axis=0,
        )

    inner_corner = lax.ppermute(corner(inner_col), "span", inner_pairs)
    outer_corner = lax.ppermute(corner(outer_col), "span", outer_pairs)
    partial = sum_stations(got, cols)
    count = lax.axis_size("chord")
    row = lax.axis_index("chord")
    half = count // 2
    pairs = [(i, 0 if i < half else count - 1) for i in (1, count - 2)]
    partial = partial + lax.ppermute(partial.astype(BF16), "chord", pairs).astype(F32)
    swap = [(0, count - 1), (count - 1, 0)]
    shed = partial + lax.ppermute(partial.astype(BF16), "chord", swap).astype(F32)
    shed = split_parts(shed)
    shed, inner_corner = lax.optimization_barrier((shed, inner_corner))
    halos = (low, high, inner, outer, inner_corner, outer_corner)
    out = surface(False, block_codes, place, own, halos, *shared, done=out)

    first = out[0].astype(F32) - jnp.where(row == 0, 1.0, 0.0) * shed
    last = out[rows - 1].astype(F32) + jnp.where(row == count - 1, 1.0, 0.0) * shed
    return out.at[0].set(first.astype(BF16)).at[rows - 1].set(last.astype(BF16))


def solution(mesh):
    in_specs = (
        P("chord", "span", None, None),
        P(None, "chord", "span", None, None),
        P(None, "chord", "span"),
        P("chord", "span", None, None, None, None),
        P("chord", "span", None),
        P(("span", "chord"), None, None),
        P(("span", "chord"), None),
        P(("span", "chord")),
    )
    out_specs = P("chord", "span", None, None)
    return jax.shard_map(
        per_device, mesh=mesh, in_specs=in_specs, out_specs=out_specs, check_vma=False
    )
```
